512 devices in a mesh: grp: 16 (over x_lo, y), row: 32 (over x_hi, z, core).
Axes of the slice: x: 4 (x_hi: 2, x_lo: 2; x = x_hi * 2 + x_lo), y: 8, z: 8, core: 2. Of those that a mesh axis runs over, the one named last changes fastest.
Arguments:
- q_proj: bfloat16 [256, 131072], P(None, ('grp', 'row')), may hold values from -6 to 6
- k_proj: bfloat16 [256, 131072], P(None, ('grp', 'row')), may hold values from -6 to 6
- v_proj: bfloat16 [256, 131072], P(None, ('grp', 'row')), may hold values from -6 to 6
- filter_spectrum: float32 [2, 32, 256, 32, 256], P(None, 'grp', None, 'row'), may hold values from -6 to 6
- skip_gain: float32 [256], replicated, may hold values from -3 to 3
Outputs:
- gated: float32 [256, 131072], P(None, ('grp', 'row'))
The draws below stay inside these ranges and needn't reach their ends.
All inputs are finite; a program needn't handle non-finite values.
Results may differ from the reference program's by a relative error of at most 0.0029.
Values may be sent and summed in bfloat16 or wider, within the bound.
No kernel may reach another device: no remote copies, remote signals or barrier semaphores. Data moves between devices by JAX's collectives and lax.ppermute only.
A program may use at most 64 MiB of HBM per device.

```python
import jax
import jax.numpy as jnp
from jax import lax

CHAN = 256
TOK_DEV = 256
TOKENS = 131072
PADDED = 262144
SPEC_LOW = 32
SPEC_MID = 32


def shard_levels(key, dims, cuts, smallest, top_value):
    def one(dim, parts):
        heights = jax.random.uniform(jax.random.fold_in(jax.random.fold_in(key, 6), dim), (parts,), jnp.float32, smallest / len(cuts), top_value / len(cuts))
        return jnp.repeat(jnp.exp(heights), dims[dim] // parts).reshape((-1,) + (1,) * (len(dims) - dim - 1))

    level = one(*cuts[0])
    for cut in cuts[1:]:
        level = level * one(*cut)
    return level


def gaussian(stream_key, extent, scale, bound, pieces=(), held_as=jnp.bfloat16):
    values = jax.random.normal(stream_key, extent, jnp.float32) * scale
    if len(pieces) > 0:
        values = shard_levels(stream_key, extent, pieces, -0.22, 0.18) * values
    return jnp.clip(values, min=-bound, max=bound).astype(held_as)


def setup_inputs(seed: int = 0) -> dict:
    keys = jax.random.split(jax.random.key(seed), 6)
    q_proj = gaussian(keys[0], (CHAN, TOKENS), 1.0, 6.0, ((1, 512),))
    k_proj = gaussian(keys[1], (CHAN, TOKENS), 1.0, 6.0, ((1, 512),))
    v_proj = gaussian(keys[2], (CHAN, TOKENS), 1.0, 6.0, ((1, 512),))
    filter_spectrum = gaussian(keys[3], (2, SPEC_LOW, CHAN, SPEC_MID, TOK_DEV), 1.0, 6.0, ((1, 16), (3, 32)), jnp.float32)
    skip_gain = gaussian(keys[4], (CHAN,), 0.5, 3.0, (), jnp.float32)
    return dict(q_proj=q_proj, k_proj=k_proj, v_proj=v_proj, filter_spectrum=filter_spectrum, skip_gain=skip_gain)


def reference(q_proj, k_proj, v_proj, filter_spectrum, skip_gain):
    product = (k_proj.astype(jnp.float32) * v_proj.astype(jnp.float32)).astype(jnp.bfloat16)
    product = lax.optimization_barrier(product)
    signal = product.astype(jnp.float32)
    block_width = 8

    def one_block(block_start):
        spectra = lax.dynamic_slice_in_dim(filter_spectrum, block_start, block_width, 2)
        spectra = jnp.transpose(spectra, (0, 2, 4, 3, 1)).reshape(2, block_width, PADDED)
        source = lax.dynamic_slice_in_dim(signal, block_start, block_width, 0)
        padded = jnp.concatenate([source, jnp.zeros_like(source)], axis=1)
        forward = jnp.fft.fft(padded, axis=1)
        response = lax.complex(spectra[0], spectra[1])
        inverse = jnp.fft.ifft(forward * response, axis=1)
        return jnp.real(inverse[:, :TOKENS])

    starts = (jnp.arange(CHAN // block_width) * block_width).astype(jnp.int32)
    conv = lax.map(one_block, starts).reshape(CHAN, TOKENS)
    return q_proj.astype(jnp.float32) * (conv + skip_gain[:, None] * signal)
```

```python
import functools
import math

import jax
import jax.numpy as jnp
import ml_dtypes
import numpy as np
from jax import lax
from jax.experimental import pallas as pl
from jax.experimental.pallas import tpu as pltpu
from jax.sharding import PartitionSpec as P

both_axes = ("grp", "row")
LANES = 128
vmem_params = pltpu.CompilerParams(vmem_limit_bytes=40 * 1024 * 1024)


def split_bf16(table):
    table = np.asarray(table, np.float32)
    high = table.astype(ml_dtypes.bfloat16)
    low = (table - high.astype(np.float32)).astype(ml_dtypes.bfloat16)
    return high, low


def unit_angles(numer, denom):
    return 2.0 * math.pi / denom * (numer % denom).astype(np.float64)


@functools.lru_cache
def tables(groups, rows, length):
    blocks = groups * rows
    padded = 2 * blocks * length
    outer = np.arange(blocks, dtype=np.int64)
    inner = np.arange(length, dtype=np.int64)
    forward, backward, twist = [], [], []
    for parity in range(2):
        low = 2 * (outer // rows) + parity + 2 * groups * (outer % rows)
        theta = unit_angles(low[:, None] * outer[None, :], 2 * blocks)
        stacked = np.concatenate([np.cos(theta), -np.sin(theta)], axis=0)
        forward.append(np.stack(split_bf16(stacked)))
        backward.append(np.stack(split_bf16(stacked.T / padded)))
        phi = unit_angles(low[:, None] * inner[None, :], padded)
        twist.append(np.stack([np.cos(phi), np.sin(phi)]).astype(np.float32))
    angle = unit_angles(inner[:, None] * inner[None, :], length)
    cosine, sine = np.cos(angle), np.sin(angle)
    inner_forward = np.stack(split_bf16(np.block([[cosine, -sine], [sine, cosine]])))
    inner_backward = np.stack(split_bf16(np.block([[cosine, sine], [-sine, cosine]])))
    return np.stack(forward), np.stack(backward), np.stack(twist), inner_forward, inner_backward


def dot(left, right):
    return jnp.dot(left, right, preferred_element_type=jnp.float32)


def halves(value):
    high = value.astype(jnp.bfloat16)
    return high, (value - high.astype(jnp.float32)).astype(jnp.bfloat16)


def pack_kernel(k_ref, v_ref, filter_ref, out_ref, wide):
    channels = k_ref.shape[0]
    for part in range(2):
        for parity in range(2):
            first = (part * 2 + parity) * 2 * channels
            for half in range(2):
                wide[pl.ds(6 * parity + 2 * part + half, channels, stride=12), :] = filter_ref[
                    pl.ds(first + half, channels, stride=2), :
                ]
    product = k_ref[...].astype(jnp.float32) * v_ref[...].astype(jnp.float32)
    product = product.astype(jnp.bfloat16).astype(jnp.float32)
    for parity in range(2):
        for half in range(2):
            wide[pl.ds(6 * parity + 4 + half, channels, stride=12), :] = product[
                :, half * LANES : (half + 1) * LANES
            ]
    out_ref[...] = wide[...].astype(jnp.bfloat16)


def transform_kernel(
    got_ref, forward_ref, backward_ref, twist_ref, inner_f_ref, inner_b_ref, out_ref, wide, narrow
):
    blocks = got_ref.shape[0] // 6
    length = 2 * LANES
    wide[...] = got_ref[...].astype(jnp.float32)

    def piece(index):
        return jnp.concatenate(
            [wide[pl.ds(2 * index + half, blocks, stride=6), :] for half in range(2)], axis=1
        )

    signal = piece(2).astype(jnp.bfloat16)
    field = dot(forward_ref[0], signal) + dot(forward_ref[1], signal)
    real, imag = field[:blocks], field[blocks:]
    cosine, sine = twist_ref[0], twist_ref[1]
    high, low = halves(
        jnp.concatenate([real * cosine + imag * sine, imag * cosine - real * sine], axis=1)
    )
    spectrum = dot(high, inner_f_ref[0]) + (dot(low, inner_f_ref[0]) + dot(high, inner_f_ref[1]))
    real, imag = spectrum[:, :length], spectrum[:, length:]
    resp_real, resp_imag = piece(0), piece(1)
    high, low = halves(
        jnp.concatenate(
            [real * resp_real - imag * resp_imag, real * resp_imag + imag * resp_real], axis=1
        )
    )
    back = dot(high, inner_b_ref[0]) + (dot(low, inner_b_ref[0]) + dot(high, inner_b_ref[1]))
    real, imag = back[:, :length], back[:, length:]
    high, low = halves(
        jnp.concatenate([real * cosine - imag * sine, imag * cosine + real * sine], axis=0)
    )
    conv = dot(backward_ref[0], high) + (dot(backward_ref[1], high) + dot(backward_ref[0], low))
    for half in range(2):
        narrow[pl.ds(half, blocks, stride=2), :] = conv[:, half * LANES : (half + 1) * LANES]
    out_ref[...] = narrow[...].astype(jnp.bfloat16)


def gate_kernel(got_ref, q_ref, k_ref, v_ref, gain_ref, out_ref, wide):
    channels = q_ref.shape[0]
    wide[...] = got_ref[...].astype(jnp.float32)
    conv = jnp.concatenate(
        [
            wide[pl.ds(half, channels, stride=4), :] + wide[pl.ds(2 + half, channels, stride=4), :]
            for half in range(2)
        ],
        axis=1,
    )
    signal = (k_ref[...].astype(jnp.float32) * v_ref[...].astype(jnp.float32)).astype(jnp.bfloat16)
    out_ref[...] = q_ref[...].astype(jnp.float32) * (
        conv + gain_ref[...] * signal.astype(jnp.float32)
    )


def body(q_proj, k_proj, v_proj, filter_spectrum, skip_gain):
    channels, length = q_proj.shape
    groups, rows = lax.axis_size("grp"), lax.axis_size("row")
    blocks = groups * rows
    parity = lax.axis_index("row") % 2
    forward, backward, twist, inner_f, inner_b = tables(groups, rows, length)

    def mine(table):
        return lax.dynamic_index_in_dim(jnp.asarray(table), parity, 0, keepdims=False)

    with jax.named_scope("pack"):
        outgoing = pl.pallas_call(
            pack_kernel,
            out_shape=jax.ShapeDtypeStruct((6 * blocks, LANES), jnp.bfloat16),
            scratch_shapes=[pltpu.VMEM((6 * blocks, LANES), jnp.float32)],
            compiler_params=vmem_params,
        )(k_proj, v_proj, filter_spectrum.reshape(8 * channels, LANES))
    with jax.named_scope("scatter_channels"):
        incoming = lax.all_to_all(
            outgoing.reshape(blocks, 3, 2, LANES), both_axes, 0, 0, tiled=True
        )
    with jax.named_scope("transform"):
        partial_conv = pl.pallas_call(
            transform_kernel,
            out_shape=jax.ShapeDtypeStruct((2 * blocks, LANES), jnp.bfloat16),
            scratch_shapes=[
                pltpu.VMEM((6 * blocks, LANES), jnp.float32),
                pltpu.VMEM((2 * blocks, LANES), jnp.float32),
            ],
            compiler_params=vmem_params,
        )(
            incoming.reshape(6 * blocks, LANES),
            mine(forward),
            mine(backward),
            mine(twist),
            jnp.asarray(inner_f),
            jnp.asarray(inner_b),
        )
    with jax.named_scope("return_positions"):
        returned = lax.all_to_all(
            partial_conv.reshape(blocks, 2, LANES), both_axes, 0, 0, tiled=True
        )
    with jax.named_scope("gate"):
        return pl.pallas_call(
            gate_kernel,
            out_shape=jax.ShapeDtypeStruct((channels, length), jnp.float32),
            scratch_shapes=[pltpu.VMEM((2 * blocks, LANES), jnp.float32)],
            compiler_params=vmem_params,
        )(returned.reshape(2 * blocks, LANES), q_proj, k_proj, v_proj, skip_gain[:, None])


def solution(mesh):
    placed = (
        P(None, ("grp", "row")),
        P(None, ("grp", "row")),
        P(None, ("grp", "row")),
        P(None, "grp", None, "row", None),
        P(),
    )
    return jax.shard_map(
        body, mesh=mesh, in_specs=placed, out_specs=P(None, ("grp", "row")), check_vma=False
    )
```

```python
import functools
import math

import jax
import jax.numpy as jnp
import ml_dtypes
import numpy as np
from jax import lax
from jax.experimental import pallas as pl
from jax.experimental.pallas import tpu as pltpu
from jax.sharding import PartitionSpec as P

both_axes = ("grp", "row")
LANES = 128
CHUNKS = 4


def split_bf16(table):
    table = np.asarray(table, np.float32)
    high = table.astype(ml_dtypes.bfloat16)
    low = (table - high.astype(np.float32)).astype(ml_dtypes.bfloat16)
    return high, low


def unit_angles(numer, denom):
    return 2.0 * math.pi / denom * (numer % denom).astype(np.float64)


@functools.lru_cache
def tables(groups, rows, length):
    blocks, padded = groups * rows, 2 * groups * rows * length
    pair = np.arange(blocks // 2, dtype=np.int64)
    group, half_row = pair // (rows // 2), pair % (rows // 2)
    inner = np.arange(length, dtype=np.int64)
    forward, backward, fine, coarse = [], [], [], []
    for core in range(2):
        low_parts = (2 * np.arange(groups)[None, :] + np.arange(2)[:, None]).reshape(-1)
        high_parts = 2 * groups * (2 * np.arange(rows // 2) + core)
        low = (low_parts[:, None] + high_parts[None, :]).reshape(-1)
        outer = group * rows + 2 * half_row + core
        theta = unit_angles(low[:, None] * outer[None, :], 2 * blocks)
        matrix = np.concatenate([np.cos(theta), -np.sin(theta)], axis=0)
        forward.append(np.stack(split_bf16(matrix)))
        backward.append(np.stack(split_bf16(matrix.T / padded)))
        steps = np.concatenate([inner, np.full(LANES, (1 - 2 * core) * length)])
        for parts, store in ((low_parts, fine), (high_parts, coarse)):
            phi = unit_angles(parts[:, None] * steps[None, :], padded)
            store.append(np.stack([np.cos(phi), np.sin(phi)]).astype(np.float32))
    angle = unit_angles(inner[:, None] * inner[None, :], length)
    cosine, sine = np.cos(angle), np.sin(angle)
    mixed = np.stack(split_bf16(np.block([[cosine, -sine], [sine, cosine]])))
    stacked = [np.stack(t) for t in (forward, fine, coarse)]
    return [*stacked, mixed], np.stack(backward)


def dot(left, right):
    return jnp.dot(left, right, preferred_element_type=jnp.float32)


def halves(value):
    high = value.astype(jnp.bfloat16)
    return high, (value - high.astype(jnp.float32)).astype(jnp.bfloat16)


def dot_wide(high, low, table):
    return dot(
        jnp.concatenate([high, low, high], axis=1),
        jnp.concatenate([table[0], table[0], table[1]], axis=0),
    )


def rotate(real, imag, cosine, sine):
    return real * cosine + imag * sine, imag * cosine - real * sine


def joined(ref, first, step, count):
    return jnp.concatenate(
        [ref[pl.ds(first + half, count, stride=step), :] for half in range(2)], axis=1
    )


def pack_kernel(k_hbm, v_hbm, filter_hbm, out_hbm, k_ref, v_ref, filter_ref, wide, out_ref, sems):
    channels = k_ref.shape[0]
    chunk = channels // CHUNKS
    fetch = [pltpu.make_async_copy(k_hbm, k_ref, sems.at[0]),
             pltpu.make_async_copy(v_hbm, v_ref, sems.at[1])]
    for index in range(CHUNKS):
        rows = pl.ds(2 * index * chunk, 2 * chunk)
        fetch.append(
            pltpu.make_async_copy(
                filter_hbm.at[:, rows], filter_ref.at[:, rows], sems.at[2 + index]
            )
        )
    for copy in fetch:
        copy.start()
    fetch[0].wait()
    fetch[1].wait()
    product = k_ref[...].astype(jnp.float32) * v_ref[...].astype(jnp.float32)
    product = product.astype(jnp.bfloat16).astype(jnp.float32)
    for half in range(2):
        wide[pl.ds(8 + half, channels, stride=10), :] = product[
            :, half * LANES : (half + 1) * LANES
        ]
    send = []
    for index in range(CHUNKS):
        fetch[2 + index].wait()
        first = 10 * index * chunk
        for part in range(2):
            for low in range(2):
                for half in range(2):
                    wide[pl.ds(first + 4 * low + 2 * part + half, chunk, stride=10), :] = (
                        filter_ref[
                            2 * part + low, pl.ds(2 * index * chunk + half, chunk, stride=2), :
                        ]
                    )
        rows = pl.ds(first, 10 * chunk)
        out_ref[rows, :] = wide[rows, :].astype(jnp.bfloat16)
        send.append(
            pltpu.make_async_copy(out_ref.at[rows], out_hbm.at[rows], sems.at[2 + CHUNKS + index])
        )
        send[index].start()
    for copy in send:
        copy.wait()


def tables_kernel(*refs):
    core = lax.axis_index("row") % 2
    count = (len(refs) - 1) // 2
    sems = refs[-1]
    copies = []
    for index in range(count):
        source = refs[index] if index == count - 1 else refs[index].at[core]
        copies.append(pltpu.make_async_copy(source, refs[count + index], sems.at[index]))
        copies[index].start()
    for copy in copies:
        copy.wait()


def own_kernel(got_ref, forward_ref, fine_ref, coarse_ref, field_ref, response_ref, twist_ref, wide):
    pairs = got_ref.shape[0] // 10
    wide[...] = got_ref[...].astype(jnp.float32)
    signal = joined(wide, 8, 10, pairs).astype(jnp.bfloat16)
    field_ref[...] = dot(forward_ref[0], signal) + dot(forward_ref[1], signal)
    for part in range(2):
        for low in range(2):
            response_ref[part, low * pairs : (low + 1) * pairs, :] = joined(
                wide, 4 * low + 2 * part, 10, pairs
            )
    count = coarse_ref.shape[1]
    cosine, sine = coarse_ref[0], coarse_ref[1]
    for index in range(fine_ref.shape[1]):
        rows = slice(index * count, (index + 1) * count)
        fine_cos, fine_sin = fine_ref[0, index : index + 1], fine_ref[1, index : index + 1]
        twist_ref[0, rows, :] = cosine * fine_cos - sine * fine_sin
        twist_ref[1, rows, :] = sine * fine_cos + cosine * fine_sin


def spectrum_kernel(
    backward_hbm, other_ref, forward_ref, field_ref, response_ref, twist_ref, mixed_ref,
    sent_ref, kept_ref, wide, backward_ref, sem,
):
    core = lax.axis_index("row") % 2
    fetch = pltpu.make_async_copy(backward_hbm.at[core], backward_ref, sem)
    fetch.start()
    pairs = other_ref.shape[0] // 2
    count, length = 2 * pairs, 2 * LANES
    wide[...] = other_ref[...].astype(jnp.float32)
    signal = joined(wide, 0, 2, pairs).astype(jnp.bfloat16)
    field = dot(forward_ref[0], signal) + dot(forward_ref[1], signal)
    shift_cos = jnp.concatenate([twist_ref[0, :, length:]] * 2, axis=1)
    shift_sin = jnp.concatenate([twist_ref[1, :, length:]] * 2, axis=1)
    cosine, sine = twist_ref[0, :, :length], twist_ref[1, :, :length]
    real, imag = rotate(field[:count], field[count:], shift_cos, shift_sin)
    real, imag = rotate(field_ref[:count] + real, field_ref[count:] + imag, cosine, sine)
    high, low = halves(jnp.concatenate([real, imag], axis=1))
    spectrum = dot_wide(high, low, mixed_ref)
    real, imag = spectrum[:, :length], spectrum[:, length:]
    resp_real, resp_imag = response_ref[0], response_ref[1]
    high, low = halves(
        jnp.concatenate(
            [real * resp_imag + imag * resp_real, real * resp_real - imag * resp_imag], axis=1
        )
    )
    back = dot_wide(high, low, mixed_ref)
    real, imag = rotate(back[:, length:], back[:, :length], cosine, -sine)
    fetch.wait()

    def positions(real, imag):
        high, low = halves(jnp.concatenate([real, imag], axis=0))
        return dot(
            jnp.concatenate([backward_ref[0], backward_ref[0], backward_ref[1]], axis=1),
            jnp.concatenate([high, low, high], axis=0),
        )

    sent_ref[...] = positions(*rotate(real, imag, shift_cos, -shift_sin))
    kept_ref[...] = positions(real, imag)


def add_kernel(kept_ref, came_ref, out_ref, wide):
    pairs = kept_ref.shape[0]
    conv = kept_ref[...] + came_ref[...]
    for half in range(2):
        wide[pl.ds(half, pairs, stride=2), :] = conv[:, half * LANES : (half + 1) * LANES]
    out_ref[...] = wide[...].astype(jnp.bfloat16)


def gate_kernel(got_ref, q_ref, k_ref, v_ref, gain_ref, out_ref, wide):
    channels = q_ref.shape[0]
    wide[...] = got_ref[...].astype(jnp.float32)
    conv = joined(wide, 0, 2, channels)
    signal = (k_ref[...].astype(jnp.float32) * v_ref[...].astype(jnp.float32)).astype(jnp.bfloat16)
    out_ref[...] = q_ref[...].astype(jnp.float32) * (
        conv + gain_ref[...] * signal.astype(jnp.float32)
    )


def call(kernel, shapes, scratch, megabytes, anywhere=0, out_anywhere=False, operands=0):
    extra = {}
    if anywhere:
        extra["in_specs"] = [pl.BlockSpec(memory_space=pl.ANY)] * anywhere
        extra["in_specs"] += [pl.BlockSpec(memory_space=pltpu.VMEM)] * (operands - anywhere)
    if out_anywhere:
        extra["out_specs"] = pl.BlockSpec(memory_space=pl.ANY)
    return pl.pallas_call(
        kernel,
        out_shape=shapes,
        scratch_shapes=scratch,
        compiler_params=pltpu.CompilerParams(vmem_limit_bytes=megabytes * 1024 * 1024),
        **extra,
    )


def body(q_proj, k_proj, v_proj, filter_spectrum, skip_gain):
    channels, length = q_proj.shape
    groups, rows = lax.axis_size("grp"), lax.axis_size("row")
    pairs = groups * rows // 2
    same_core = [list(range(c, groups * rows, 2)) for c in range(2)]
    swap = [(i, i ^ 1) for i in range(rows)]
    f32, bf16 = jnp.float32, jnp.bfloat16
    shape = jax.ShapeDtypeStruct

    def exchange(tensor, pieces):
        return lax.all_to_all(
            tensor.reshape(pairs, pieces, 2, LANES), both_axes, 0, 0,
            tiled=True, axis_index_groups=same_core,
        )

    with jax.named_scope("pack"):
        outgoing = call(
            pack_kernel, shape((10 * channels, LANES), bf16),
            [pltpu.VMEM((channels, length), bf16)] * 2
            + [pltpu.VMEM((4, 2 * channels, LANES), f32), pltpu.VMEM((10 * channels, LANES), f32),
               pltpu.VMEM((10 * channels, LANES), bf16), pltpu.SemaphoreType.DMA((2 + 2 * CHUNKS,))],
            58, 3, True,
        )(k_proj, v_proj, filter_spectrum.reshape(4, 2 * channels, LANES))
    constants, backward = tables(groups, rows, length)
    constants = [jnp.asarray(table) for table in constants]
    outgoing, constants = lax.optimization_barrier((outgoing, constants))
    with jax.named_scope("to_channels"):
        incoming = exchange(outgoing, 5)
    with jax.named_scope("tables"):
        local = [shape(t.shape[1:], t.dtype) for t in constants[:-1]]
        local.append(shape(constants[-1].shape, constants[-1].dtype))
        parts = call(
            tables_kernel, local, [pltpu.SemaphoreType.DMA((len(local),))], 12, len(local)
        )(*constants)
    incoming, parts = lax.optimization_barrier((incoming, parts))
    forward, fine, coarse, mixed = parts
    with jax.named_scope("signal_swap"):
        other = lax.ppermute(incoming[:, 4].reshape(2 * pairs, LANES), "row", swap)
    with jax.named_scope("own_positions"):
        field, response, twist = call(
            own_kernel,
            [shape((4 * pairs, length), f32), shape((2, 2 * pairs, length), f32),
             shape((2, 2 * pairs, length + LANES), f32)],
            [pltpu.VMEM((10 * pairs, LANES), f32)], 8,
        )(incoming.reshape(10 * pairs, LANES), forward, fine, coarse)
    with jax.named_scope("spectrum"):
        sent, kept = call(
            spectrum_kernel, [shape((pairs, length), f32)] * 2,
            [pltpu.VMEM((2 * pairs, LANES), f32), pltpu.VMEM(backward.shape[1:], bf16),
             pltpu.SemaphoreType.DMA], 20, 1, operands=7,
        )(jnp.asarray(backward), other, forward, field, response, twist, mixed)
    with jax.named_scope("result_swap"):
        came = lax.ppermute(sent, "row", swap)
    with jax.named_scope("add_cores"):
        result = call(
            add_kernel, shape((2 * pairs, LANES), bf16), [pltpu.VMEM((2 * pairs, LANES), f32)], 4
        )(kept, came)
    with jax.named_scope("to_positions"):
        returned = exchange(result, 1)
    with jax.named_scope("gate"):
        return call(
            gate_kernel, shape((channels, length), f32),
            [pltpu.VMEM((2 * channels, LANES), f32)], 4,
        )(returned.reshape(2 * channels, LANES), q_proj, k_proj, v_proj, skip_gain[:, None])


def solution(mesh):
    placed = (
        P(None, ("grp", "row")),
        P(None, ("grp", "row")),
        P(None, ("grp", "row")),
        P(None, "grp", None, "row", None),
        P(),
    )
    return jax.shard_map(
        body, mesh=mesh, in_specs=placed, out_specs=P(None, ("grp", "row")), check_vma=False
    )
```

```python
import functools
import math

import jax
import jax.numpy as jnp
import ml_dtypes
import numpy as np
from jax import lax
from jax.experimental import pallas as pl
from jax.experimental.pallas import tpu as pltpu
from jax.sharding import PartitionSpec as P

both_axes = ("grp", "row")
LANES = 128
CHUNKS = 4


def split_bf16(table):
    table = np.asarray(table, np.float32)
    high = table.astype(ml_dtypes.bfloat16)
    low = (table - high.astype(np.float32)).astype(ml_dtypes.bfloat16)
    return high, low


def unit_angles(numer, denom):
    return 2.0 * math.pi / denom * (numer % denom).astype(np.float64)


def group_order(groups, rows):
    halves = rows // 2
    group_list = [(groups // 4 - i) % groups for i in range(groups)]
    half_list = [(13 * halves // 16 - i) % halves for i in range(halves)]
    return group_list, half_list


@functools.lru_cache
def tables(groups, rows, length):
    blocks, padded = groups * rows, 2 * groups * rows * length
    group_list, half_list = (np.array(t, np.int64) for t in group_order(groups, rows))
    inner = np.arange(length, dtype=np.int64)
    forward, backward, fine, coarse = [], [], [], []
    for core in range(2):
        low_parts = (2 * group_list[None, :] + np.arange(2)[:, None]).reshape(-1)
        high_parts = 2 * groups * (2 * half_list + core)
        low = (low_parts[:, None] + high_parts[None, :]).reshape(-1)
        outer = (group_list[:, None] * rows + 2 * half_list[None, :] + core).reshape(-1)
        theta = unit_angles(low[:, None] * outer[None, :], 2 * blocks)
        matrix = np.concatenate([np.cos(theta), -np.sin(theta)], axis=0)
        forward.append(np.stack(split_bf16(matrix)))
        backward.append(np.stack(split_bf16(matrix.T / padded)))
        steps = np.concatenate([inner, np.full(LANES, (1 - 2 * core) * length)])
        for parts, store in ((low_parts, fine), (high_parts, coarse)):
            phi = unit_angles(parts[:, None] * steps[None, :], padded)
            store.append(np.stack([np.cos(phi), np.sin(phi)]).astype(np.float32))
    angle = unit_angles(inner[:, None] * inner[None, :], length)
    cosine, sine = np.cos(angle), np.sin(angle)
    mixed = np.stack(split_bf16(np.block([[cosine, -sine], [sine, cosine]])))
    stacked = [np.stack(t) for t in (forward, fine, coarse)]
    return [*stacked, mixed], np.stack(backward)


def dot(left, right):
    return jnp.dot(left, right, preferred_element_type=jnp.float32)


def halves(value):
    high = value.astype(jnp.bfloat16)
    return high, (value - high.astype(jnp.float32)).astype(jnp.bfloat16)


def dot_wide(high, low, table):
    return dot(
        jnp.concatenate([high, low, high], axis=1),
        jnp.concatenate([table[0], table[0], table[1]], axis=0),
    )


def rotate(real, imag, cosine, sine):
    return real * cosine + imag * sine, imag * cosine - real * sine


def joined(ref, first, step, count):
    return jnp.concatenate(
        [ref[pl.ds(first + half, count, stride=step), :] for half in range(2)], axis=1
    )


def pack_kernel(k_hbm, v_hbm, filter_hbm, out_hbm, k_ref, v_ref, filter_ref, wide, out_ref, sems):
    channels = k_ref.shape[0]
    chunk = channels // CHUNKS
    fetch = [pltpu.make_async_copy(k_hbm, k_ref, sems.at[0]),
             pltpu.make_async_copy(v_hbm, v_ref, sems.at[1])]
    for index in range(CHUNKS):
        rows = pl.ds(2 * index * chunk, 2 * chunk)
        fetch.append(
            pltpu.make_async_copy(
                filter_hbm.at[:, rows], filter_ref.at[:, rows], sems.at[2 + index]
            )
        )
    for copy in fetch:
        copy.start()
    fetch[0].wait()
    fetch[1].wait()
    product = k_ref[...].astype(jnp.float32) * v_ref[...].astype(jnp.float32)
    product = product.astype(jnp.bfloat16).astype(jnp.float32)
    for half in range(2):
        wide[pl.ds(8 + half, channels, stride=10), :] = product[
            :, half * LANES : (half + 1) * LANES
        ]
    send = []
    for index in range(CHUNKS):
        fetch[2 + index].wait()
        first = 10 * index * chunk
        for part in range(2):
            for low in range(2):
                for half in range(2):
                    wide[pl.ds(first + 4 * low + 2 * part + half, chunk, stride=10), :] = (
                        filter_ref[
                            2 * part + low, pl.ds(2 * index * chunk + half, chunk, stride=2), :
                        ]
                    )
        rows = pl.ds(first, 10 * chunk)
        out_ref[rows, :] = wide[rows, :].astype(jnp.bfloat16)
        send.append(
            pltpu.make_async_copy(out_ref.at[rows], out_hbm.at[rows], sems.at[2 + CHUNKS + index])
        )
        send[index].start()
    for copy in send:
        copy.wait()


def tables_kernel(*refs):
    core = lax.axis_index("row") % 2
    count = (len(refs) - 1) // 2
    sems = refs[-1]
    copies = []
    for index in range(count):
        source = refs[index] if index == count - 1 else refs[index].at[core]
        copies.append(pltpu.make_async_copy(source, refs[count + index], sems.at[index]))
        copies[index].start()
    for copy in copies:
        copy.wait()


def own_kernel(got_ref, forward_ref, fine_ref, coarse_ref, field_ref, response_ref, twist_ref, wide):
    pairs = got_ref.shape[0] // 10
    wide[...] = got_ref[...].astype(jnp.float32)
    signal = joined(wide, 8, 10, pairs).astype(jnp.bfloat16)
    field_ref[...] = dot(forward_ref[0], signal) + dot(forward_ref[1], signal)
    for part in range(2):
        for low in range(2):
            response_ref[part, low * pairs : (low + 1) * pairs, :] = joined(
                wide, 4 * low + 2 * part, 10, pairs
            )
    count = coarse_ref.shape[1]
    cosine, sine = coarse_ref[0], coarse_ref[1]
    for index in range(fine_ref.shape[1]):
        rows = slice(index * count, (index + 1) * count)
        fine_cos, fine_sin = fine_ref[0, index : index + 1], fine_ref[1, index : index + 1]
        twist_ref[0, rows, :] = cosine * fine_cos - sine * fine_sin
        twist_ref[1, rows, :] = sine * fine_cos + cosine * fine_sin


def spectrum_kernel(
    backward_hbm, other_ref, forward_ref, field_ref, response_ref, twist_ref, mixed_ref,
    sent_ref, kept_ref, wide, backward_ref, sem,
):
    core = lax.axis_index("row") % 2
    fetch = pltpu.make_async_copy(backward_hbm.at[core], backward_ref, sem)
    fetch.start()
    pairs = other_ref.shape[0] // 2
    count, length = 2 * pairs, 2 * LANES
    wide[...] = other_ref[...].astype(jnp.float32)
    signal = joined(wide, 0, 2, pairs).astype(jnp.bfloat16)
    field = dot(forward_ref[0], signal) + dot(forward_ref[1], signal)
    shift_cos = jnp.concatenate([twist_ref[0, :, length:]] * 2, axis=1)
    shift_sin = jnp.concatenate([twist_ref[1, :, length:]] * 2, axis=1)
    cosine, sine = twist_ref[0, :, :length], twist_ref[1, :, :length]
    real, imag = rotate(field[:count], field[count:], shift_cos, shift_sin)
    real, imag = rotate(field_ref[:count] + real, field_ref[count:] + imag, cosine, sine)
    high, low = halves(jnp.concatenate([real, imag], axis=1))
    spectrum = dot_wide(high, low, mixed_ref)
    real, imag = spectrum[:, :length], spectrum[:, length:]
    resp_real, resp_imag = response_ref[0], response_ref[1]
    high, low = halves(
        jnp.concatenate(
            [real * resp_imag + imag * resp_real, real * resp_real - imag * resp_imag], axis=1
        )
    )
    back = dot_wide(high, low, mixed_ref)
    real, imag = rotate(back[:, length:], back[:, :length], cosine, -sine)
    fetch.wait()

    def positions(real, imag):
        high, low = halves(jnp.concatenate([real, imag], axis=0))
        return dot(
            jnp.concatenate([backward_ref[0], backward_ref[0], backward_ref[1]], axis=1),
            jnp.concatenate([high, low, high], axis=0),
        )

    sent_ref[...] = positions(*rotate(real, imag, shift_cos, -shift_sin))
    kept_ref[...] = positions(real, imag)


def add_kernel(kept_ref, came_ref, out_ref, wide):
    pairs = kept_ref.shape[0]
    conv = kept_ref[...] + came_ref[...]
    for half in range(2):
        wide[pl.ds(half, pairs, stride=2), :] = conv[:, half * LANES : (half + 1) * LANES]
    out_ref[...] = wide[...].astype(jnp.bfloat16)


def gate_kernel(got_ref, q_ref, k_ref, v_ref, gain_ref, out_ref, wide):
    channels = q_ref.shape[0]
    wide[...] = got_ref[...].astype(jnp.float32)
    conv = joined(wide, 0, 2, channels)
    signal = (k_ref[...].astype(jnp.float32) * v_ref[...].astype(jnp.float32)).astype(jnp.bfloat16)
    out_ref[...] = q_ref[...].astype(jnp.float32) * (
        conv + gain_ref[...] * signal.astype(jnp.float32)
    )


def call(kernel, shapes, scratch, megabytes, anywhere=0, out_anywhere=False, operands=0):
    extra = {}
    if anywhere:
        extra["in_specs"] = [pl.BlockSpec(memory_space=pl.ANY)] * anywhere
        extra["in_specs"] += [pl.BlockSpec(memory_space=pltpu.VMEM)] * (operands - anywhere)
    if out_anywhere:
        extra["out_specs"] = pl.BlockSpec(memory_space=pl.ANY)
    return pl.pallas_call(
        kernel,
        out_shape=shapes,
        scratch_shapes=scratch,
        compiler_params=pltpu.CompilerParams(vmem_limit_bytes=megabytes * 1024 * 1024),
        **extra,
    )


def body(q_proj, k_proj, v_proj, filter_spectrum, skip_gain):
    channels, length = q_proj.shape
    groups, rows = lax.axis_size("grp"), lax.axis_size("row")
    pairs = groups * rows // 2
    group_list, half_list = group_order(groups, rows)
    same_core = [[g * rows + 2 * i + c for g in group_list for i in half_list] for c in range(2)]
    swap = [(i, i ^ 1) for i in range(rows)]
    f32, bf16 = jnp.float32, jnp.bfloat16
    shape = jax.ShapeDtypeStruct

    def exchange(tensor, pieces):
        return lax.all_to_all(
            tensor.reshape(pairs, pieces, 2, LANES), both_axes, 0, 0,
            tiled=True, axis_index_groups=same_core,
        )

    with jax.named_scope("pack"):
        outgoing = call(
            pack_kernel, shape((10 * channels, LANES), bf16),
            [pltpu.VMEM((channels, length), bf16)] * 2
            + [pltpu.VMEM((4, 2 * channels, LANES), f32), pltpu.VMEM((10 * channels, LANES), f32),
               pltpu.VMEM((10 * channels, LANES), bf16), pltpu.SemaphoreType.DMA((2 + 2 * CHUNKS,))],
            58, 3, True,
        )(k_proj, v_proj, filter_spectrum.reshape(4, 2 * channels, LANES))
    constants, backward = tables(groups, rows, length)
    constants = [jnp.asarray(table) for table in constants]
    outgoing, constants = lax.optimization_barrier((outgoing, constants))
    with jax.named_scope("to_channels"):
        incoming = exchange(outgoing, 5)
    with jax.named_scope("tables"):
        local = [shape(t.shape[1:], t.dtype) for t in constants[:-1]]
        local.append(shape(constants[-1].shape, constants[-1].dtype))
        parts = call(
            tables_kernel, local, [pltpu.SemaphoreType.DMA((len(local),))], 12, len(local)
        )(*constants)
    incoming, parts = lax.optimization_barrier((incoming, parts))
    forward, fine, coarse, mixed = parts
    with jax.named_scope("signal_swap"):
        other = lax.ppermute(incoming[:, 4].reshape(2 * pairs, LANES), "row", swap)
    with jax.named_scope("own_positions"):
        field, response, twist = call(
            own_kernel,
            [shape((4 * pairs, length), f32), shape((2, 2 * pairs, length), f32),
             shape((2, 2 * pairs, length + LANES), f32)],
            [pltpu.VMEM((10 * pairs, LANES), f32)], 8,
        )(incoming.reshape(10 * pairs, LANES), forward, fine, coarse)
    with jax.named_scope("spectrum"):
        sent, kept = call(
            spectrum_kernel, [shape((pairs, length), f32)] * 2,
            [pltpu.VMEM((2 * pairs, LANES), f32), pltpu.VMEM(backward.shape[1:], bf16),
             pltpu.SemaphoreType.DMA], 20, 1, operands=7,
        )(jnp.asarray(backward), other, forward, field, response, twist, mixed)
    with jax.named_scope("result_swap"):
        came = lax.ppermute(sent, "row", swap)
    with jax.named_scope("add_cores"):
        result = call(
            add_kernel, shape((2 * pairs, LANES), bf16), [pltpu.VMEM((2 * pairs, LANES), f32)], 4
        )(kept, came)
    with jax.named_scope("to_positions"):
        returned = exchange(result, 1)
    with jax.named_scope("gate"):
        return call(
            gate_kernel, shape((channels, length), f32),
            [pltpu.VMEM((2 * channels, LANES), f32)], 4,
        )(returned.reshape(2 * channels, LANES), q_proj, k_proj, v_proj, skip_gain[:, None])


def solution(mesh):
    placed = (
        P(None, ("grp", "row")),
        P(None, ("grp", "row")),
        P(None, ("grp", "row")),
        P(None, "grp", None, "row", None),
        P(),
    )
    return jax.shard_map(
        body, mesh=mesh, in_specs=placed, out_specs=P(None, ("grp", "row")), check_vma=False
    )
```

```python
import functools
import math

import jax
import jax.numpy as jnp
import ml_dtypes
import numpy as np
from jax import lax
from jax.experimental import pallas as pl
from jax.experimental.pallas import tpu as pltpu
from jax.sharding import PartitionSpec as P

both_axes = ("grp", "row")
LANES = 128
CHUNKS = 4


def split_bf16(table):
    table = np.asarray(table, np.float32)
    high = table.astype(ml_dtypes.bfloat16)
    low = (table - high.astype(np.float32)).astype(ml_dtypes.bfloat16)
    return high, low


def unit_angles(numer, denom):
    return 2.0 * math.pi / denom * (numer % denom).astype(np.float64)


def group_order(groups, rows):
    ring, halves = groups // 2, rows // 2
    first_group, first_half = groups // 4, 13 * halves // 16

    def nearness(group):
        place = group % ring
        return min(place, ring - place), place, group

    group_list = sorted((g for g in range(groups) if g != first_group), key=nearness)
    half_list = sorted(
        (i for i in range(halves) if i != first_half),
        key=lambda i: (-(i % (halves // 2)), -i),
    )
    return [first_group, *group_list], [first_half, *half_list]


@functools.lru_cache
def tables(groups, rows, length):
    blocks, padded = groups * rows, 2 * groups * rows * length
    group_list, half_list = (np.array(t, np.int64) for t in group_order(groups, rows))
    inner = np.arange(length, dtype=np.int64)
    forward, backward, fine, coarse = [], [], [], []
    for core in range(2):
        low_parts = (2 * group_list[None, :] + np.arange(2)[:, None]).reshape(-1)
        high_parts = 2 * groups * (2 * half_list + core)
        low = (low_parts[:, None] + high_parts[None, :]).reshape(-1)
        outer = (group_list[:, None] * rows + 2 * half_list[None, :] + core).reshape(-1)
        theta = unit_angles(low[:, None] * outer[None, :], 2 * blocks)
        matrix = np.concatenate([np.cos(theta), -np.sin(theta)], axis=0)
        forward.append(np.stack(split_bf16(matrix)))
        backward.append(np.stack(split_bf16(matrix.T / padded)))
        steps = np.concatenate([inner, np.full(LANES, (1 - 2 * core) * length)])
        for parts, store in ((low_parts, fine), (high_parts, coarse)):
            phi = unit_angles(parts[:, None] * steps[None, :], padded)
            store.append(np.stack([np.cos(phi), np.sin(phi)]).astype(np.float32))
    angle = unit_angles(inner[:, None] * inner[None, :], length)
    cosine, sine = np.cos(angle), np.sin(angle)
    mixed = np.stack(split_bf16(np.block([[cosine, -sine], [sine, cosine]])))
    stacked = [np.stack(t) for t in (forward, fine, coarse)]
    return [*stacked, mixed], np.stack(backward)


def dot(left, right):
    return jnp.dot(left, right, preferred_element_type=jnp.float32)


def halves(value):
    high = value.astype(jnp.bfloat16)
    return high, (value - high.astype(jnp.float32)).astype(jnp.bfloat16)


def dot_wide(high, low, table):
    return dot(
        jnp.concatenate([high, low, high], axis=1),
        jnp.concatenate([table[0], table[0], table[1]], axis=0),
    )


def rotate(real, imag, cosine, sine):
    return real * cosine + imag * sine, imag * cosine - real * sine


def joined(ref, first, step, count):
    return jnp.concatenate(
        [ref[pl.ds(first + half, count, stride=step), :] for half in range(2)], axis=1
    )


def pack_kernel(k_hbm, v_hbm, filter_hbm, out_hbm, k_ref, v_ref, filter_ref, wide, out_ref, sems):
    channels = k_ref.shape[0]
    chunk = channels // CHUNKS
    fetch = [pltpu.make_async_copy(k_hbm, k_ref, sems.at[0]),
             pltpu.make_async_copy(v_hbm, v_ref, sems.at[1])]
    for index in range(CHUNKS):
        rows = pl.ds(2 * index * chunk, 2 * chunk)
        fetch.append(
            pltpu.make_async_copy(
                filter_hbm.at[:, rows], filter_ref.at[:, rows], sems.at[2 + index]
            )
        )
    for copy in fetch:
        copy.start()
    fetch[0].wait()
    fetch[1].wait()
    product = k_ref[...].astype(jnp.float32) * v_ref[...].astype(jnp.float32)
    product = product.astype(jnp.bfloat16).astype(jnp.float32)
    for half in range(2):
        wide[pl.ds(8 + half, channels, stride=10), :] = product[
            :, half * LANES : (half + 1) * LANES
        ]
    send = []
    for index in range(CHUNKS):
        fetch[2 + index].wait()
        first = 10 * index * chunk
        for part in range(2):
            for low in range(2):
                for half in range(2):
                    wide[pl.ds(first + 4 * low + 2 * part + half, chunk, stride=10), :] = (
                        filter_ref[
                            2 * part + low, pl.ds(2 * index * chunk + half, chunk, stride=2), :
                        ]
                    )
        rows = pl.ds(first, 10 * chunk)
        out_ref[rows, :] = wide[rows, :].astype(jnp.bfloat16)
        send.append(
            pltpu.make_async_copy(out_ref.at[rows], out_hbm.at[rows], sems.at[2 + CHUNKS + index])
        )
        send[index].start()
    for copy in send:
        copy.wait()


def tables_kernel(*refs):
    core = lax.axis_index("row") % 2
    count = (len(refs) - 1) // 2
    sems = refs[-1]
    copies = []
    for index in range(count):
        source = refs[index] if index == count - 1 else refs[index].at[core]
        copies.append(pltpu.make_async_copy(source, refs[count + index], sems.at[index]))
        copies[index].start()
    for copy in copies:
        copy.wait()


def own_kernel(got_ref, forward_ref, fine_ref, coarse_ref, field_ref, response_ref, twist_ref, wide):
    pairs = got_ref.shape[0] // 10
    wide[...] = got_ref[...].astype(jnp.float32)
    signal = joined(wide, 8, 10, pairs).astype(jnp.bfloat16)
    field_ref[...] = dot(forward_ref[0], signal) + dot(forward_ref[1], signal)
    for part in range(2):
        for low in range(2):
            response_ref[part, low * pairs : (low + 1) * pairs, :] = joined(
                wide, 4 * low + 2 * part, 10, pairs
            )
    count = coarse_ref.shape[1]
    cosine, sine = coarse_ref[0], coarse_ref[1]
    for index in range(fine_ref.shape[1]):
        rows = slice(index * count, (index + 1) * count)
        fine_cos, fine_sin = fine_ref[0, index : index + 1], fine_ref[1, index : index + 1]
        twist_ref[0, rows, :] = cosine * fine_cos - sine * fine_sin
        twist_ref[1, rows, :] = sine * fine_cos + cosine * fine_sin


def spectrum_kernel(
    backward_hbm, other_ref, forward_ref, field_ref, response_ref, twist_ref, mixed_ref,
    sent_ref, kept_ref, wide, backward_ref, sem,
):
    core = lax.axis_index("row") % 2
    fetch = pltpu.make_async_copy(backward_hbm.at[core], backward_ref, sem)
    fetch.start()
    pairs = other_ref.shape[0] // 2
    count, length = 2 * pairs, 2 * LANES
    wide[...] = other_ref[...].astype(jnp.float32)
    signal = joined(wide, 0, 2, pairs).astype(jnp.bfloat16)
    field = dot(forward_ref[0], signal) + dot(forward_ref[1], signal)
    shift_cos = jnp.concatenate([twist_ref[0, :, length:]] * 2, axis=1)
    shift_sin = jnp.concatenate([twist_ref[1, :, length:]] * 2, axis=1)
    cosine, sine = twist_ref[0, :, :length], twist_ref[1, :, :length]
    real, imag = rotate(field[:count], field[count:], shift_cos, shift_sin)
    real, imag = rotate(field_ref[:count] + real, field_ref[count:] + imag, cosine, sine)
    high, low = halves(jnp.concatenate([real, imag], axis=1))
    spectrum = dot_wide(high, low, mixed_ref)
    real, imag = spectrum[:, :length], spectrum[:, length:]
    resp_real, resp_imag = response_ref[0], response_ref[1]
    high, low = halves(
        jnp.concatenate(
            [real * resp_imag + imag * resp_real, real * resp_real - imag * resp_imag], axis=1
        )
    )
    back = dot_wide(high, low, mixed_ref)
    real, imag = rotate(back[:, length:], back[:, :length], cosine, -sine)
    fetch.wait()

    def positions(real, imag):
        high, low = halves(jnp.concatenate([real, imag], axis=0))
        return dot(
            jnp.concatenate([backward_ref[0], backward_ref[0], backward_ref[1]], axis=1),
            jnp.concatenate([high, low, high], axis=0),
        )

    sent_ref[...] = positions(*rotate(real, imag, shift_cos, -shift_sin))
    kept_ref[...] = positions(real, imag)


def add_kernel(kept_ref, came_ref, out_ref, wide):
    pairs = kept_ref.shape[0]
    conv = kept_ref[...] + came_ref[...]
    for half in range(2):
        wide[pl.ds(half, pairs, stride=2), :] = conv[:, half * LANES : (half + 1) * LANES]
    out_ref[...] = wide[...].astype(jnp.bfloat16)


def gate_kernel(got_ref, q_ref, k_ref, v_ref, gain_ref, out_ref, wide):
    channels = q_ref.shape[0]
    wide[...] = got_ref[...].astype(jnp.float32)
    conv = joined(wide, 0, 2, channels)
    signal = (k_ref[...].astype(jnp.float32) * v_ref[...].astype(jnp.float32)).astype(jnp.bfloat16)
    out_ref[...] = q_ref[...].astype(jnp.float32) * (
        conv + gain_ref[...] * signal.astype(jnp.float32)
    )


def call(kernel, shapes, scratch, megabytes, anywhere=0, out_anywhere=False, operands=0):
    extra = {}
    if anywhere:
        extra["in_specs"] = [pl.BlockSpec(memory_space=pl.ANY)] * anywhere
        extra["in_specs"] += [pl.BlockSpec(memory_space=pltpu.VMEM)] * (operands - anywhere)
    if out_anywhere:
        extra["out_specs"] = pl.BlockSpec(memory_space=pl.ANY)
    return pl.pallas_call(
        kernel,
        out_shape=shapes,
        scratch_shapes=scratch,
        compiler_params=pltpu.CompilerParams(vmem_limit_bytes=megabytes * 1024 * 1024),
        **extra,
    )


def body(q_proj, k_proj, v_proj, filter_spectrum, skip_gain):
    channels, length = q_proj.shape
    groups, rows = lax.axis_size("grp"), lax.axis_size("row")
    pairs = groups * rows // 2
    group_list, half_list = group_order(groups, rows)
    same_core = [[g * rows + 2 * i + c for g in group_list for i in half_list] for c in range(2)]
    swap = [(i, i ^ 1) for i in range(rows)]
    f32, bf16 = jnp.float32, jnp.bfloat16
    shape = jax.ShapeDtypeStruct

    def exchange(tensor, pieces):
        return lax.all_to_all(
            tensor.reshape(pairs, pieces, 2, LANES), both_axes, 0, 0,
            tiled=True, axis_index_groups=same_core,
        )

    with jax.named_scope("pack"):
        outgoing = call(
            pack_kernel, shape((10 * channels, LANES), bf16),
            [pltpu.VMEM((channels, length), bf16)] * 2
            + [pltpu.VMEM((4, 2 * channels, LANES), f32), pltpu.VMEM((10 * channels, LANES), f32),
               pltpu.VMEM((10 * channels, LANES), bf16), pltpu.SemaphoreType.DMA((2 + 2 * CHUNKS,))],
            58, 3, True,
        )(k_proj, v_proj, filter_spectrum.reshape(4, 2 * channels, LANES))
    constants, backward = tables(groups, rows, length)
    constants = [jnp.asarray(table) for table in constants]
    outgoing, constants = lax.optimization_barrier((outgoing, constants))
    with jax.named_scope("to_channels"):
        incoming = exchange(outgoing, 5)
    with jax.named_scope("tables"):
        local = [shape(t.shape[1:], t.dtype) for t in constants[:-1]]
        local.append(shape(constants[-1].shape, constants[-1].dtype))
        parts = call(
            tables_kernel, local, [pltpu.SemaphoreType.DMA((len(local),))], 12, len(local)
        )(*constants)
    incoming, parts = lax.optimization_barrier((incoming, parts))
    forward, fine, coarse, mixed = parts
    with jax.named_scope("signal_swap"):
        other = lax.ppermute(incoming[:, 4].reshape(2 * pairs, LANES), "row", swap)
    with jax.named_scope("own_positions"):
        field, response, twist = call(
            own_kernel,
            [shape((4 * pairs, length), f32), shape((2, 2 * pairs, length), f32),
             shape((2, 2 * pairs, length + LANES), f32)],
            [pltpu.VMEM((10 * pairs, LANES), f32)], 8,
        )(incoming.reshape(10 * pairs, LANES), forward, fine, coarse)
    with jax.named_scope("spectrum"):
        sent, kept = call(
            spectrum_kernel, [shape((pairs, length), f32)] * 2,
            [pltpu.VMEM((2 * pairs, LANES), f32), pltpu.VMEM(backward.shape[1:], bf16),
             pltpu.SemaphoreType.DMA], 20, 1, operands=7,
        )(jnp.asarray(backward), other, forward, field, response, twist, mixed)
    with jax.named_scope("result_swap"):
        came = lax.ppermute(sent, "row", swap)
    with jax.named_scope("add_cores"):
        result = call(
            add_kernel, shape((2 * pairs, LANES), bf16), [pltpu.VMEM((2 * pairs, LANES), f32)], 4
        )(kept, came)
    with jax.named_scope("to_positions"):
        returned = exchange(result, 1)
    with jax.named_scope("gate"):
        return call(
            gate_kernel, shape((channels, length), f32),
            [pltpu.VMEM((2 * channels, LANES), f32)], 4,
        )(returned.reshape(2 * channels, LANES), q_proj, k_proj, v_proj, skip_gain[:, None])


def solution(mesh):
    placed = (
        P(None, ("grp", "row")),
        P(None, ("grp", "row")),
        P(None, ("grp", "row")),
        P(None, "grp", None, "row", None),
        P(),
    )
    return jax.shard_map(
        body, mesh=mesh, in_specs=placed, out_specs=P(None, ("grp", "row")), check_vma=False
    )
```

```python
import functools
import math

import jax
import jax.numpy as jnp
import ml_dtypes
import numpy as np
from jax import lax
from jax.experimental import pallas as pl
from jax.experimental.pallas import tpu as pltpu
from jax.sharding import PartitionSpec as P

both_axes = ("grp", "row")
LANES = 128
CHUNKS = 4
SPARE = 16


def split_bf16(table):
    table = np.asarray(table, np.float32)
    high = table.astype(ml_dtypes.bfloat16)
    low = (table - high.astype(np.float32)).astype(ml_dtypes.bfloat16)
    return high, low


def unit_angles(numer, denom):
    return 2.0 * math.pi / denom * (numer % denom).astype(np.float64)


def group_order(groups, rows):
    ring, halves = groups // 2, rows // 2
    first_group, first_half = groups // 4, 13 * halves // 16

    def nearness(group):
        place = group % ring
        return min(place, ring - place), place, group

    group_list = sorted((g for g in range(groups) if g != first_group), key=nearness)
    half_list = sorted(
        (i for i in range(halves) if i != first_half),
        key=lambda i: (-(i % (halves // 2)), -i),
    )
    return [first_group, *group_list], [first_half, *half_list]


@functools.lru_cache
def tables(groups, rows, length):
    blocks, padded = groups * rows, 2 * groups * rows * length
    group_list, half_list = (np.array(t, np.int64) for t in group_order(groups, rows))
    inner = np.arange(length, dtype=np.int64)
    forward, backward, fine, coarse = [], [], [], []
    for core in range(2):
        low_parts = (2 * group_list[None, :] + np.arange(2)[:, None]).reshape(-1)
        high_parts = 2 * groups * (2 * half_list + core)
        low = (low_parts[:, None] + high_parts[None, :]).reshape(-1)
        outer = (group_list[:, None] * rows + 2 * half_list[None, :] + core).reshape(-1)
        theta = unit_angles(low[:, None] * outer[None, :], 2 * blocks)
        matrix = np.concatenate([np.cos(theta), -np.sin(theta)], axis=0)
        forward.append(np.stack(split_bf16(matrix)))
        backward.append(np.stack(split_bf16(matrix.T / padded)))
        steps = np.concatenate([inner, np.full(LANES, (1 - 2 * core) * length)])
        for parts, store in ((low_parts, fine), (high_parts, coarse)):
            phi = unit_angles(parts[:, None] * steps[None, :], padded)
            store.append(np.stack([np.cos(phi), np.sin(phi)]).astype(np.float32))
    angle = unit_angles(inner[:, None] * inner[None, :], length)
    cosine, sine = np.cos(angle), np.sin(angle)
    mixed = np.stack(split_bf16(np.block([[cosine, -sine], [sine, cosine]])))
    stacked = [np.stack(t) for t in (forward, fine, coarse)]
    return [*stacked, mixed], np.stack(backward)


def dot(left, right):
    return jnp.dot(left, right, preferred_element_type=jnp.float32)


def halves(value):
    high = value.astype(jnp.bfloat16)
    return high, (value - high.astype(jnp.float32)).astype(jnp.bfloat16)


def dot_wide(high, low, table):
    return dot(
        jnp.concatenate([high, low, high], axis=1),
        jnp.concatenate([table[0], table[0], table[1]], axis=0),
    )


def rotate(real, imag, cosine, sine):
    return real * cosine + imag * sine, imag * cosine - real * sine


def joined(ref, first, step, count):
    return jnp.concatenate(
        [ref[pl.ds(first + half, count, stride=step), :] for half in range(2)], axis=1
    )


def pack_kernel(k_hbm, v_hbm, filter_hbm, out_hbm, k_ref, v_ref, filter_ref, wide, out_ref, sems):
    channels = k_ref.shape[0]
    chunk = channels // CHUNKS
    fetch = [pltpu.make_async_copy(k_hbm, k_ref, sems.at[0]),
             pltpu.make_async_copy(v_hbm, v_ref, sems.at[1])]
    for index in range(CHUNKS):
        rows = pl.ds(2 * index * chunk, 2 * chunk)
        fetch.append(
            pltpu.make_async_copy(
                filter_hbm.at[:, rows], filter_ref.at[:, rows], sems.at[2 + index]
            )
        )
    for copy in fetch:
        copy.start()
    fetch[0].wait()
    fetch[1].wait()
    product = k_ref[...].astype(jnp.float32) * v_ref[...].astype(jnp.float32)
    product = product.astype(jnp.bfloat16).astype(jnp.float32)
    for half in range(2):
        wide[pl.ds(8 + half, channels, stride=10), :] = product[
            :, half * LANES : (half + 1) * LANES
        ]
    send = []
    for index in range(CHUNKS):
        fetch[2 + index].wait()
        first = 10 * index * chunk
        for part in range(2):
            for low in range(2):
                for half in range(2):
                    wide[pl.ds(first + 4 * low + 2 * part + half, chunk, stride=10), :] = (
                        filter_ref[
                            2 * part + low, pl.ds(2 * index * chunk + half, chunk, stride=2), :
                        ]
                    )
        rows = pl.ds(first, 10 * chunk)
        out_ref[rows, :] = wide[rows, :].astype(jnp.bfloat16)
        send.append(
            pltpu.make_async_copy(out_ref.at[rows], out_hbm.at[rows], sems.at[2 + CHUNKS + index])
        )
        send[index].start()
    for copy in send:
        copy.wait()


def tables_kernel(*refs):
    core = lax.axis_index("row") % 2
    count = (len(refs) - 1) // 2
    sems = refs[-1]
    copies = []
    for index in range(count):
        source = refs[index] if index == count - 1 else refs[index].at[core]
        copies.append(pltpu.make_async_copy(source, refs[count + index], sems.at[index]))
        copies[index].start()
    for copy in copies:
        copy.wait()


def own_kernel(got_ref, forward_ref, fine_ref, coarse_ref, field_ref, response_ref, twist_ref, wide):
    pairs = got_ref.shape[0] // 10
    wide[: got_ref.shape[0], :] = got_ref[...].astype(jnp.float32)
    signal = joined(wide, 8, 10, pairs).astype(jnp.bfloat16)
    field_ref[...] = dot(forward_ref[0], signal) + dot(forward_ref[1], signal)
    for part in range(2):
        for low in range(2):
            response_ref[part, low * pairs : (low + 1) * pairs, :] = joined(
                wide, 4 * low + 2 * part, 10, pairs
            )
    count = coarse_ref.shape[1]
    cosine, sine = coarse_ref[0], coarse_ref[1]
    for index in range(fine_ref.shape[1]):
        rows = slice(index * count, (index + 1) * count)
        fine_cos, fine_sin = fine_ref[0, index : index + 1], fine_ref[1, index : index + 1]
        twist_ref[0, rows, :] = cosine * fine_cos - sine * fine_sin
        twist_ref[1, rows, :] = sine * fine_cos + cosine * fine_sin


def spectrum_kernel(
    backward_hbm, other_ref, forward_ref, field_ref, response_ref, twist_ref, mixed_ref,
    sent_ref, kept_ref, wide, backward_ref, sem,
):
    core = lax.axis_index("row") % 2
    fetch = pltpu.make_async_copy(backward_hbm.at[core], backward_ref, sem)
    fetch.start()
    pairs = other_ref.shape[0] // 2
    count, length = 2 * pairs, 2 * LANES
    wide[: other_ref.shape[0], :] = other_ref[...].astype(jnp.float32)
    signal = joined(wide, 0, 2, pairs).astype(jnp.bfloat16)
    field = dot(forward_ref[0], signal) + dot(forward_ref[1], signal)
    shift_cos = jnp.concatenate([twist_ref[0, :, length:]] * 2, axis=1)
    shift_sin = jnp.concatenate([twist_ref[1, :, length:]] * 2, axis=1)
    cosine, sine = twist_ref[0, :, :length], twist_ref[1, :, :length]
    real, imag = rotate(field[:count], field[count:], shift_cos, shift_sin)
    real, imag = rotate(field_ref[:count] + real, field_ref[count:] + imag, cosine, sine)
    high, low = halves(jnp.concatenate([real, imag], axis=1))
    spectrum = dot_wide(high, low, mixed_ref)
    real, imag = spectrum[:, :length], spectrum[:, length:]
    resp_real, resp_imag = response_ref[0], response_ref[1]
    high, low = halves(
        jnp.concatenate(
            [real * resp_imag + imag * resp_real, real * resp_real - imag * resp_imag], axis=1
        )
    )
    back = dot_wide(high, low, mixed_ref)
    real, imag = rotate(back[:, length:], back[:, :length], cosine, -sine)
    fetch.wait()

    def positions(real, imag):
        high, low = halves(jnp.concatenate([real, imag], axis=0))
        return dot(
            jnp.concatenate([backward_ref[0], backward_ref[0], backward_ref[1]], axis=1),
            jnp.concatenate([high, low, high], axis=0),
        )

    sent_ref[...] = positions(*rotate(real, imag, shift_cos, -shift_sin))
    kept_ref[...] = positions(real, imag)


def add_kernel(kept_ref, came_ref, out_ref, wide):
    pairs = kept_ref.shape[0]
    conv = kept_ref[...] + came_ref[...]
    for half in range(2):
        wide[pl.ds(half, pairs, stride=2), :] = conv[:, half * LANES : (half + 1) * LANES]
    out_ref[...] = wide[: out_ref.shape[0], :].astype(jnp.bfloat16)


def gate_kernel(got_ref, q_ref, k_ref, v_ref, gain_ref, out_ref, wide):
    channels = q_ref.shape[0]
    wide[: got_ref.shape[0], :] = got_ref[...].astype(jnp.float32)
    conv = joined(wide, 0, 2, channels)
    signal = (k_ref[...].astype(jnp.float32) * v_ref[...].astype(jnp.float32)).astype(jnp.bfloat16)
    out_ref[...] = q_ref[...].astype(jnp.float32) * (
        conv + gain_ref[...] * signal.astype(jnp.float32)
    )


def call(kernel, shapes, scratch, megabytes, anywhere=0, out_anywhere=False, operands=0):
    extra = {}
    if anywhere:
        extra["in_specs"] = [pl.BlockSpec(memory_space=pl.ANY)] * anywhere
        extra["in_specs"] += [pl.BlockSpec(memory_space=pltpu.VMEM)] * (operands - anywhere)
    if out_anywhere:
        extra["out_specs"] = pl.BlockSpec(memory_space=pl.ANY)
    return pl.pallas_call(
        kernel,
        out_shape=shapes,
        scratch_shapes=scratch,
        compiler_params=pltpu.CompilerParams(vmem_limit_bytes=megabytes * 1024 * 1024),
        **extra,
    )


def body(q_proj, k_proj, v_proj, filter_spectrum, skip_gain):
    channels, length = q_proj.shape
    groups, rows = lax.axis_size("grp"), lax.axis_size("row")
    pairs = groups * rows // 2
    group_list, half_list = group_order(groups, rows)
    same_core = [[g * rows + 2 * i + c for g in group_list for i in half_list] for c in range(2)]
    swap = [(i, i ^ 1) for i in range(rows)]
    f32, bf16 = jnp.float32, jnp.bfloat16
    shape = jax.ShapeDtypeStruct

    def exchange(tensor, pieces):
        return lax.all_to_all(
            tensor.reshape(pairs, pieces, 2, LANES), both_axes, 0, 0,
            tiled=True, axis_index_groups=same_core,
        )

    with jax.named_scope("pack"):
        outgoing = call(
            pack_kernel, shape((10 * channels, LANES), bf16),
            [pltpu.VMEM((channels, length), bf16)] * 2
            + [pltpu.VMEM((4, 2 * channels + SPARE, LANES), f32),
               pltpu.VMEM((10 * channels + SPARE, LANES), f32),
               pltpu.VMEM((10 * channels, LANES), bf16), pltpu.SemaphoreType.DMA((2 + 2 * CHUNKS,))],
            58, 3, True,
        )(k_proj, v_proj, filter_spectrum.reshape(4, 2 * channels, LANES))
    constants, backward = tables(groups, rows, length)
    constants = [jnp.asarray(table) for table in constants]
    outgoing, constants = lax.optimization_barrier((outgoing, constants))
    with jax.named_scope("to_channels"):
        incoming = exchange(outgoing, 5)
    with jax.named_scope("tables"):
        local = [shape(t.shape[1:], t.dtype) for t in constants[:-1]]
        local.append(shape(constants[-1].shape, constants[-1].dtype))
        parts = call(
            tables_kernel, local, [pltpu.SemaphoreType.DMA((len(local),))], 12, len(local)
        )(*constants)
    incoming, parts = lax.optimization_barrier((incoming, parts))
    forward, fine, coarse, mixed = parts
    with jax.named_scope("signal_swap"):
        other = lax.ppermute(incoming[:, 4].reshape(2 * pairs, LANES), "row", swap)
    with jax.named_scope("own_positions"):
        field, response, twist = call(
            own_kernel,
            [shape((4 * pairs, length), f32), shape((2, 2 * pairs, length), f32),
             shape((2, 2 * pairs, length + LANES), f32)],
            [pltpu.VMEM((10 * pairs + SPARE, LANES), f32)], 8,
        )(incoming.reshape(10 * pairs, LANES), forward, fine, coarse)
    with jax.named_scope("spectrum"):
        sent, kept = call(
            spectrum_kernel, [shape((pairs, length), f32)] * 2,
            [pltpu.VMEM((2 * pairs + SPARE, LANES), f32), pltpu.VMEM(backward.shape[1:], bf16),
             pltpu.SemaphoreType.DMA], 20, 1, operands=7,
        )(jnp.asarray(backward), other, forward, field, response, twist, mixed)
    with jax.named_scope("result_swap"):
        came = lax.ppermute(sent, "row", swap)
    with jax.named_scope("add_cores"):
        result = call(
            add_kernel, shape((2 * pairs, LANES), bf16),
            [pltpu.VMEM((2 * pairs + SPARE, LANES), f32)], 4
        )(kept, came)
    with jax.named_scope("to_positions"):
        returned = exchange(result, 1)
    with jax.named_scope("gate"):
        return call(
            gate_kernel, shape((channels, length), f32),
            [pltpu.VMEM((2 * channels + SPARE, LANES), f32)], 4,
        )(returned.reshape(2 * channels, LANES), q_proj, k_proj, v_proj, skip_gain[:, None])


def solution(mesh):
    placed = (
        P(None, ("grp", "row")),
        P(None, ("grp", "row")),
        P(None, ("grp", "row")),
        P(None, "grp", None, "row", None),
        P(),
    )
    return jax.shard_map(
        body, mesh=mesh, in_specs=placed, out_specs=P(None, ("grp", "row")), check_vma=False
    )
```

```python
import functools
import math

import jax
import jax.numpy as jnp
import ml_dtypes
import numpy as np
from jax import lax
from jax.experimental import pallas as pl
from jax.experimental.pallas import tpu as pltpu
from jax.sharding import PartitionSpec as P

both_axes = ("grp", "row")
LANES = 128
CHUNKS = 4
SPARE = 16


def split_bf16(table):
    table = np.asarray(table, np.float32)
    high = table.astype(ml_dtypes.bfloat16)
    low = (table - high.astype(np.float32)).astype(ml_dtypes.bfloat16)
    return high, low


def unit_angles(numer, denom):
    return 2.0 * math.pi / denom * (numer % denom).astype(np.float64)


def group_order(groups, rows):
    ring, halves = groups // 2, rows // 2
    first_group, first_half = groups // 4, 13 * halves // 16

    def nearness(group):
        place = group % ring
        return min(place, ring - place), place, group

    group_list = sorted((g for g in range(groups) if g != first_group), key=nearness)
    half_list = sorted(
        (i for i in range(halves) if i != first_half),
        key=lambda i: (-(i % (halves // 2)), -i),
    )
    return [first_group, *group_list], [first_half, *half_list]


@functools.lru_cache
def tables(groups, rows, length):
    blocks, padded = groups * rows, 2 * groups * rows * length
    group_list, half_list = (np.array(t, np.int64) for t in group_order(groups, rows))
    inner = np.arange(length, dtype=np.int64)
    forward, backward, fine, coarse = [], [], [], []
    for core in range(2):
        low_parts = (2 * group_list[None, :] + np.arange(2)[:, None]).reshape(-1)
        high_parts = 2 * groups * (2 * half_list + core)
        low = (low_parts[:, None] + high_parts[None, :]).reshape(-1)
        outer = (group_list[:, None] * rows + 2 * half_list[None, :] + core).reshape(-1)
        theta = unit_angles(low[:, None] * outer[None, :], 2 * blocks)
        matrix = np.concatenate([np.cos(theta), -np.sin(theta)], axis=0)
        forward.append(np.stack(split_bf16(matrix)))
        backward.append(np.stack(split_bf16(matrix.T / padded)))
        steps = np.concatenate([inner, np.full(LANES, (1 - 2 * core) * length)])
        for parts, store in ((low_parts, fine), (high_parts, coarse)):
            phi = unit_angles(parts[:, None] * steps[None, :], padded)
            store.append(np.stack([np.cos(phi), np.sin(phi)]).astype(np.float32))
    angle = unit_angles(inner[:, None] * inner[None, :], length)
    cosine, sine = np.cos(angle), np.sin(angle)
    mixed = np.stack(split_bf16(np.block([[cosine, -sine], [sine, cosine]])))
    stacked = [np.stack(t) for t in (forward, fine, coarse)]
    return [*stacked, mixed], np.stack(backward)


def dot(left, right):
    return jnp.dot(left, right, preferred_element_type=jnp.float32)


def halves(value):
    high = value.astype(jnp.bfloat16)
    return high, (value - high.astype(jnp.float32)).astype(jnp.bfloat16)


def dot_wide(high, low, table):
    return dot(
        jnp.concatenate([high, low, high], axis=1),
        jnp.concatenate([table[0], table[0], table[1]], axis=0),
    )


def rotate(real, imag, cosine, sine):
    return real * cosine + imag * sine, imag * cosine - real * sine


def joined(ref, first, step, count):
    return jnp.concatenate(
        [ref[pl.ds(first + half, count, stride=step), :] for half in range(2)], axis=1
    )


def pack_kernel(k_hbm, v_hbm, filter_hbm, out_hbm, k_ref, v_ref, filter_ref, wide, out_ref, sems):
    channels = k_ref.shape[0]
    chunk = channels // CHUNKS
    fetch = [pltpu.make_async_copy(k_hbm, k_ref, sems.at[0]),
             pltpu.make_async_copy(v_hbm, v_ref, sems.at[1])]
    for index in range(CHUNKS):
        rows = pl.ds(2 * index * chunk, 2 * chunk)
        fetch.append(
            pltpu.make_async_copy(
                filter_hbm.at[:, rows], filter_ref.at[:, rows], sems.at[2 + index]
            )
        )
    for copy in fetch:
        copy.start()
    fetch[0].wait()
    fetch[1].wait()
    product = k_ref[...].astype(jnp.float32) * v_ref[...].astype(jnp.float32)
    product = product.astype(jnp.bfloat16).astype(jnp.float32)
    for half in range(2):
        wide[pl.ds(8 + half, channels, stride=10), :] = product[
            :, half * LANES : (half + 1) * LANES
        ]
    send = []
    for index in range(CHUNKS):
        fetch[2 + index].wait()
        first = 10 * index * chunk
        for part in range(2):
            for low in range(2):
                for half in range(2):
                    wide[pl.ds(first + 4 * low + 2 * part + half, chunk, stride=10), :] = (
                        filter_ref[
                            2 * part + low, pl.ds(2 * index * chunk + half, chunk, stride=2), :
                        ]
                    )
        rows = pl.ds(first, 10 * chunk)
        out_ref[rows, :] = wide[rows, :].astype(jnp.bfloat16)
        send.append(
            pltpu.make_async_copy(out_ref.at[rows], out_hbm.at[rows], sems.at[2 + CHUNKS + index])
        )
        send[index].start()
    for copy in send:
        copy.wait()


def tables_kernel(*refs):
    core = lax.axis_index("row") % 2
    count = (len(refs) - 1) // 2
    sems = refs[-1]
    copies = []
    for index in range(count):
        source = refs[index] if index == count - 1 else refs[index].at[core]
        copies.append(pltpu.make_async_copy(source, refs[count + index], sems.at[index]))
        copies[index].start()
    for copy in copies:
        copy.wait()


def own_kernel(got_ref, forward_ref, fine_ref, coarse_ref, field_ref, response_ref, twist_ref, wide):
    pairs = got_ref.shape[0] // 10
    wide[: got_ref.shape[0], :] = got_ref[...].astype(jnp.float32)
    signal = joined(wide, 8, 10, pairs).astype(jnp.bfloat16)
    field_ref[...] = dot(forward_ref[0], signal) + dot(forward_ref[1], signal)
    for part in range(2):
        for low in range(2):
            response_ref[part, low * pairs : (low + 1) * pairs, :] = joined(
                wide, 4 * low + 2 * part, 10, pairs
            )
    count = coarse_ref.shape[1]
    cosine, sine = coarse_ref[0], coarse_ref[1]
    for index in range(fine_ref.shape[1]):
        rows = slice(index * count, (index + 1) * count)
        fine_cos, fine_sin = fine_ref[0, index : index + 1], fine_ref[1, index : index + 1]
        twist_ref[0, rows, :] = cosine * fine_cos - sine * fine_sin
        twist_ref[1, rows, :] = sine * fine_cos + cosine * fine_sin


def spectrum_kernel(
    backward_hbm, other_ref, forward_ref, field_ref, response_ref, twist_ref, mixed_ref,
    sent_ref, kept_ref, wide, backward_ref, sem,
):
    core = lax.axis_index("row") % 2
    fetch = pltpu.make_async_copy(backward_hbm.at[core], backward_ref, sem)
    fetch.start()
    pairs = other_ref.shape[0] // 2
    count, length = 2 * pairs, 2 * LANES
    wide[: other_ref.shape[0], :] = other_ref[...].astype(jnp.float32)
    signal = joined(wide, 0, 2, pairs).astype(jnp.bfloat16)
    field = dot(forward_ref[0], signal) + dot(forward_ref[1], signal)
    shift_cos = jnp.concatenate([twist_ref[0, :, length:]] * 2, axis=1)
    shift_sin = jnp.concatenate([twist_ref[1, :, length:]] * 2, axis=1)
    cosine, sine = twist_ref[0, :, :length], twist_ref[1, :, :length]
    real, imag = rotate(field[:count], field[count:], shift_cos, shift_sin)
    real, imag = rotate(field_ref[:count] + real, field_ref[count:] + imag, cosine, sine)
    high, low = halves(jnp.concatenate([real, imag], axis=1))
    spectrum = dot_wide(high, low, mixed_ref)
    real, imag = spectrum[:, :length], spectrum[:, length:]
    resp_real, resp_imag = response_ref[0], response_ref[1]
    high, low = halves(
        jnp.concatenate(
            [real * resp_imag + imag * resp_real, real * resp_real - imag * resp_imag], axis=1
        )
    )
    back = dot_wide(high, low, mixed_ref)
    real, imag = rotate(back[:, length:], back[:, :length], cosine, -sine)
    fetch.wait()

    def positions(real, imag):
        high, low = halves(jnp.concatenate([real, imag], axis=0))
        return dot(
            jnp.concatenate([backward_ref[0], backward_ref[0], backward_ref[1]], axis=1),
            jnp.concatenate([high, low, high], axis=0),
        )

    sent_ref[...] = positions(*rotate(real, imag, shift_cos, -shift_sin))
    kept_ref[...] = positions(real, imag)


def add_kernel(kept_ref, came_ref, out_ref, wide):
    pairs = kept_ref.shape[0]
    conv = kept_ref[...] + came_ref[...]
    for half in range(2):
        wide[pl.ds(half, pairs, stride=2), :] = conv[:, half * LANES : (half + 1) * LANES]
    out_ref[...] = wide[: out_ref.shape[0], :].astype(jnp.bfloat16)


def gate_kernel(got_ref, q_ref, k_ref, v_ref, gain_ref, out_hbm, wide, out_ref, sems):
    chunk = q_ref.shape[0] // CHUNKS
    send = []
    for index in range(CHUNKS):
        rows = slice(index * chunk, (index + 1) * chunk)
        both = slice(2 * index * chunk, 2 * (index + 1) * chunk)
        wide[both, :] = got_ref[both, :].astype(jnp.float32)
        conv = joined(wide, 2 * index * chunk, 2, chunk)
        signal = k_ref[rows, :].astype(jnp.float32) * v_ref[rows, :].astype(jnp.float32)
        signal = signal.astype(jnp.bfloat16).astype(jnp.float32)
        out_ref[rows, :] = q_ref[rows, :].astype(jnp.float32) * (conv + gain_ref[rows, :] * signal)
        part = pl.ds(index * chunk, chunk)
        send.append(
            pltpu.make_async_copy(out_ref.at[part], out_hbm.at[part], sems.at[index])
        )
        send[index].start()
    for copy in send:
        copy.wait()


def call(kernel, shapes, scratch, megabytes, anywhere=0, out_anywhere=False, operands=0):
    extra = {}
    if anywhere:
        extra["in_specs"] = [pl.BlockSpec(memory_space=pl.ANY)] * anywhere
        extra["in_specs"] += [pl.BlockSpec(memory_space=pltpu.VMEM)] * (operands - anywhere)
    if out_anywhere:
        extra["out_specs"] = pl.BlockSpec(memory_space=pl.ANY)
    return pl.pallas_call(
        kernel,
        out_shape=shapes,
        scratch_shapes=scratch,
        compiler_params=pltpu.CompilerParams(vmem_limit_bytes=megabytes * 1024 * 1024),
        **extra,
    )


def body(q_proj, k_proj, v_proj, filter_spectrum, skip_gain):
    channels, length = q_proj.shape
    groups, rows = lax.axis_size("grp"), lax.axis_size("row")
    pairs = groups * rows // 2
    group_list, half_list = group_order(groups, rows)
    same_core = [[g * rows + 2 * i + c for g in group_list for i in half_list] for c in range(2)]
    swap = [(i, i ^ 1) for i in range(rows)]
    f32, bf16 = jnp.float32, jnp.bfloat16
    shape = jax.ShapeDtypeStruct

    def exchange(tensor, pieces):
        return lax.all_to_all(
            tensor.reshape(pairs, pieces, 2, LANES), both_axes, 0, 0,
            tiled=True, axis_index_groups=same_core,
        )

    with jax.named_scope("pack"):
        outgoing = call(
            pack_kernel, shape((10 * channels, LANES), bf16),
            [pltpu.VMEM((channels, length), bf16)] * 2
            + [pltpu.VMEM((4, 2 * channels + SPARE, LANES), f32),
               pltpu.VMEM((10 * channels + SPARE, LANES), f32),
               pltpu.VMEM((10 * channels, LANES), bf16), pltpu.SemaphoreType.DMA((2 + 2 * CHUNKS,))],
            58, 3, True,
        )(k_proj, v_proj, filter_spectrum.reshape(4, 2 * channels, LANES))
    constants, backward = tables(groups, rows, length)
    constants = [jnp.asarray(table) for table in constants]
    outgoing, constants = lax.optimization_barrier((outgoing, constants))
    with jax.named_scope("to_channels"):
        incoming = exchange(outgoing, 5)
    with jax.named_scope("tables"):
        local = [shape(t.shape[1:], t.dtype) for t in constants[:-1]]
        local.append(shape(constants[-1].shape, constants[-1].dtype))
        parts = call(
            tables_kernel, local, [pltpu.SemaphoreType.DMA((len(local),))], 12, len(local)
        )(*constants)
    incoming, parts = lax.optimization_barrier((incoming, parts))
    forward, fine, coarse, mixed = parts
    with jax.named_scope("signal_swap"):
        other = lax.ppermute(incoming[:, 4].reshape(2 * pairs, LANES), "row", swap)
    with jax.named_scope("own_positions"):
        field, response, twist = call(
            own_kernel,
            [shape((4 * pairs, length), f32), shape((2, 2 * pairs, length), f32),
             shape((2, 2 * pairs, length + LANES), f32)],
            [pltpu.VMEM((10 * pairs + SPARE, LANES), f32)], 8,
        )(incoming.reshape(10 * pairs, LANES), forward, fine, coarse)
    with jax.named_scope("spectrum"):
        sent, kept = call(
            spectrum_kernel, [shape((pairs, length), f32)] * 2,
            [pltpu.VMEM((2 * pairs + SPARE, LANES), f32), pltpu.VMEM(backward.shape[1:], bf16),
             pltpu.SemaphoreType.DMA], 20, 1, operands=7,
        )(jnp.asarray(backward), other, forward, field, response, twist, mixed)
    with jax.named_scope("result_swap"):
        came = lax.ppermute(sent, "row", swap)
    with jax.named_scope("add_cores"):
        result = call(
            add_kernel, shape((2 * pairs, LANES), bf16),
            [pltpu.VMEM((2 * pairs + SPARE, LANES), f32)], 4
        )(kept, came)
    with jax.named_scope("to_positions"):
        returned = exchange(result, 1)
    with jax.named_scope("gate"):
        return call(
            gate_kernel, shape((channels, length), f32),
            [pltpu.VMEM((2 * channels + SPARE, LANES), f32), pltpu.VMEM((channels, length), f32),
             pltpu.SemaphoreType.DMA((CHUNKS,))], 4, out_anywhere=True,
        )(returned.reshape(2 * channels, LANES), q_proj, k_proj, v_proj, skip_gain[:, None])


def solution(mesh):
    placed = (
        P(None, ("grp", "row")),
        P(None, ("grp", "row")),
        P(None, ("grp", "row")),
        P(None, "grp", None, "row", None),
        P(),
    )
    return jax.shard_map(
        body, mesh=mesh, in_specs=placed, out_specs=P(None, ("grp", "row")), check_vma=False
    )
```

```python
import functools
import math

import jax
import jax.numpy as jnp
import ml_dtypes
import numpy as np
from jax import lax
from jax.experimental import pallas as pl
from jax.experimental.pallas import tpu as pltpu
from jax.sharding import PartitionSpec as P

both_axes = ("grp", "row")
LANES = 128
CHUNKS = 4
SPARE = 16


def split_bf16(table):
    table = np.asarray(table, np.float32)
    high = table.astype(ml_dtypes.bfloat16)
    low = (table - high.astype(np.float32)).astype(ml_dtypes.bfloat16)
    return high, low


def unit_angles(numer, denom):
    return 2.0 * math.pi / denom * (numer % denom).astype(np.float64)


def group_order(groups, rows):
    ring, halves = groups // 2, rows // 2
    first_group, first_half = groups // 4, 13 * halves // 16

    def nearness(group):
        place = group % ring
        return min(place, ring - place), place, group

    group_list = sorted((g for g in range(groups) if g != first_group), key=nearness)
    half_list = sorted(
        (i for i in range(halves) if i != first_half),
        key=lambda i: (-(i % (halves // 2)), -i),
    )
    return [first_group, *group_list], [first_half, *half_list]


@functools.lru_cache
def tables(groups, rows, length):
    blocks, padded = groups * rows, 2 * groups * rows * length
    group_list, half_list = (np.array(t, np.int64) for t in group_order(groups, rows))
    inner = np.arange(length, dtype=np.int64)
    forward, backward, fine, coarse = [], [], [], []
    for core in range(2):
        low_parts = (2 * group_list[None, :] + np.arange(2)[:, None]).reshape(-1)
        high_parts = 2 * groups * (2 * half_list + core)
        low = (low_parts[:, None] + high_parts[None, :]).reshape(-1)
        outer = (group_list[:, None] * rows + 2 * half_list[None, :] + core).reshape(-1)
        theta = unit_angles(low[:, None] * outer[None, :], 2 * blocks)
        matrix = np.concatenate([np.cos(theta), -np.sin(theta)], axis=0)
        forward.append(np.stack(split_bf16(matrix)))
        backward.append(np.stack(split_bf16(matrix.T / padded)))
        steps = np.concatenate([inner, np.full(LANES, (1 - 2 * core) * length)])
        for parts, store in ((low_parts, fine), (high_parts, coarse)):
            phi = unit_angles(parts[:, None] * steps[None, :], padded)
            store.append(np.stack([np.cos(phi), np.sin(phi)]).astype(np.float32))
    angle = unit_angles(inner[:, None] * inner[None, :], length)
    cosine, sine = np.cos(angle), np.sin(angle)
    mixed = np.stack(split_bf16(np.block([[cosine, -sine], [sine, cosine]])))
    stacked = [np.stack(t) for t in (forward, fine, coarse)]
    return [*stacked, mixed], np.stack(backward)


def dot(left, right):
    return jnp.dot(left, right, preferred_element_type=jnp.float32)


def halves(value):
    high = value.astype(jnp.bfloat16)
    return high, (value - high.astype(jnp.float32)).astype(jnp.bfloat16)


def dot_wide(high, low, table):
    return dot(
        jnp.concatenate([high, low, high], axis=1),
        jnp.concatenate([table[0], table[0], table[1]], axis=0),
    )


def rotate(real, imag, cosine, sine):
    return real * cosine + imag * sine, imag * cosine - real * sine


def joined(ref, first, step, count):
    return jnp.concatenate(
        [ref[pl.ds(first + half, count, stride=step), :] for half in range(2)], axis=1
    )


def pack_kernel(k_hbm, v_hbm, filter_hbm, out_hbm, k_ref, v_ref, filter_ref, wide, out_ref, sems):
    channels = k_ref.shape[0]
    chunk = channels // CHUNKS
    fetch = [pltpu.make_async_copy(k_hbm, k_ref, sems.at[0]),
             pltpu.make_async_copy(v_hbm, v_ref, sems.at[1])]
    for index in range(CHUNKS):
        rows = pl.ds(2 * index * chunk, 2 * chunk)
        fetch.append(
            pltpu.make_async_copy(
                filter_hbm.at[:, rows], filter_ref.at[:, rows], sems.at[2 + index]
            )
        )
    for copy in fetch:
        copy.start()
    fetch[0].wait()
    fetch[1].wait()
    send = []
    for index in range(CHUNKS):
        fetch[2 + index].wait()
        first = 10 * index * chunk
        mine = slice(index * chunk, (index + 1) * chunk)
        product = k_ref[mine, :].astype(jnp.float32) * v_ref[mine, :].astype(jnp.float32)
        for half in range(2):
            wide[pl.ds(first + 8 + half, chunk, stride=10), :] = product[
                :, half * LANES : (half + 1) * LANES
            ]
        for part in range(2):
            for low in range(2):
                for half in range(2):
                    wide[pl.ds(first + 4 * low + 2 * part + half, chunk, stride=10), :] = (
                        filter_ref[
                            2 * part + low, pl.ds(2 * index * chunk + half, chunk, stride=2), :
                        ]
                    )
        rows = pl.ds(first, 10 * chunk)
        out_ref[rows, :] = wide[rows, :].astype(jnp.bfloat16)
        send.append(
            pltpu.make_async_copy(out_ref.at[rows], out_hbm.at[rows], sems.at[2 + CHUNKS + index])
        )
        send[index].start()
    for copy in send:
        copy.wait()


def tables_kernel(*refs):
    core = lax.axis_index("row") % 2
    count = (len(refs) - 1) // 2
    sems = refs[-1]
    copies = []
    for index in range(count):
        source = refs[index] if index == count - 1 else refs[index].at[core]
        copies.append(pltpu.make_async_copy(source, refs[count + index], sems.at[index]))
        copies[index].start()
    for copy in copies:
        copy.wait()


def own_kernel(got_ref, forward_ref, fine_ref, coarse_ref, field_ref, response_ref, twist_ref, wide):
    pairs = got_ref.shape[0] // 10
    wide[: got_ref.shape[0], :] = got_ref[...].astype(jnp.float32)
    signal = joined(wide, 8, 10, pairs).astype(jnp.bfloat16)
    field_ref[...] = dot(forward_ref[0], signal) + dot(forward_ref[1], signal)
    for part in range(2):
        for low in range(2):
            response_ref[part, low * pairs : (low + 1) * pairs, :] = joined(
                wide, 4 * low + 2 * part, 10, pairs
            )
    count = coarse_ref.shape[1]
    cosine, sine = coarse_ref[0], coarse_ref[1]
    for index in range(fine_ref.shape[1]):
        rows = slice(index * count, (index + 1) * count)
        fine_cos, fine_sin = fine_ref[0, index : index + 1], fine_ref[1, index : index + 1]
        twist_ref[0, rows, :] = cosine * fine_cos - sine * fine_sin
        twist_ref[1, rows, :] = sine * fine_cos + cosine * fine_sin


def spectrum_kernel(
    backward_hbm, other_ref, forward_ref, field_ref, response_ref, twist_ref, mixed_ref,
    sent_ref, kept_ref, wide, backward_ref, sem,
):
    core = lax.axis_index("row") % 2
    fetch = pltpu.make_async_copy(backward_hbm.at[core], backward_ref, sem)
    fetch.start()
    pairs = other_ref.shape[0] // 2
    count, length = 2 * pairs, 2 * LANES
    wide[: other_ref.shape[0], :] = other_ref[...].astype(jnp.float32)
    signal = joined(wide, 0, 2, pairs).astype(jnp.bfloat16)
    field = dot(forward_ref[0], signal) + dot(forward_ref[1], signal)
    shift_cos = jnp.concatenate([twist_ref[0, :, length:]] * 2, axis=1)
    shift_sin = jnp.concatenate([twist_ref[1, :, length:]] * 2, axis=1)
    cosine, sine = twist_ref[0, :, :length], twist_ref[1, :, :length]
    real, imag = rotate(field[:count], field[count:], shift_cos, shift_sin)
    real, imag = rotate(field_ref[:count] + real, field_ref[count:] + imag, cosine, sine)
    high, low = halves(jnp.concatenate([real, imag], axis=1))
    spectrum = dot_wide(high, low, mixed_ref)
    real, imag = spectrum[:, :length], spectrum[:, length:]
    resp_real, resp_imag = response_ref[0], response_ref[1]
    high, low = halves(
        jnp.concatenate(
            [real * resp_imag + imag * resp_real, real * resp_real - imag * resp_imag], axis=1
        )
    )
    back = dot_wide(high, low, mixed_ref)
    real, imag = rotate(back[:, length:], back[:, :length], cosine, -sine)
    fetch.wait()

    def positions(real, imag):
        high, low = halves(jnp.concatenate([real, imag], axis=0))
        return dot(
            jnp.concatenate([backward_ref[0], backward_ref[0], backward_ref[1]], axis=1),
            jnp.concatenate([high, low, high], axis=0),
        )

    sent_ref[...] = positions(*rotate(real, imag, shift_cos, -shift_sin))
    kept_ref[...] = positions(real, imag)


def add_kernel(kept_ref, came_ref, out_ref, wide):
    pairs = kept_ref.shape[0]
    conv = kept_ref[...] + came_ref[...]
    for half in range(2):
        wide[pl.ds(half, pairs, stride=2), :] = conv[:, half * LANES : (half + 1) * LANES]
    out_ref[...] = wide[: out_ref.shape[0], :].astype(jnp.bfloat16)


def gate_kernel(got_ref, q_ref, k_ref, v_ref, gain_ref, out_hbm, wide, out_ref, sems):
    chunk = q_ref.shape[0] // CHUNKS
    send = []
    for index in range(CHUNKS):
        rows = slice(index * chunk, (index + 1) * chunk)
        both = slice(2 * index * chunk, 2 * (index + 1) * chunk)
        wide[both, :] = got_ref[both, :].astype(jnp.float32)
        conv = joined(wide, 2 * index * chunk, 2, chunk)
        signal = k_ref[rows, :].astype(jnp.float32) * v_ref[rows, :].astype(jnp.float32)
        signal = signal.astype(jnp.bfloat16).astype(jnp.float32)
        out_ref[rows, :] = q_ref[rows, :].astype(jnp.float32) * (conv + gain_ref[rows, :] * signal)
        part = pl.ds(index * chunk, chunk)
        send.append(
            pltpu.make_async_copy(out_ref.at[part], out_hbm.at[part], sems.at[index])
        )
        send[index].start()
    for copy in send:
        copy.wait()


def call(kernel, shapes, scratch, megabytes, anywhere=0, out_anywhere=False, operands=0):
    extra = {}
    if anywhere:
        extra["in_specs"] = [pl.BlockSpec(memory_space=pl.ANY)] * anywhere
        extra["in_specs"] += [pl.BlockSpec(memory_space=pltpu.VMEM)] * (operands - anywhere)
    if out_anywhere:
        extra["out_specs"] = pl.BlockSpec(memory_space=pl.ANY)
    return pl.pallas_call(
        kernel,
        out_shape=shapes,
        scratch_shapes=scratch,
        compiler_params=pltpu.CompilerParams(vmem_limit_bytes=megabytes * 1024 * 1024),
        **extra,
    )


def body(q_proj, k_proj, v_proj, filter_spectrum, skip_gain):
    channels, length = q_proj.shape
    groups, rows = lax.axis_size("grp"), lax.axis_size("row")
    pairs = groups * rows // 2
    group_list, half_list = group_order(groups, rows)
    same_core = [[g * rows + 2 * i + c for g in group_list for i in half_list] for c in range(2)]
    swap = [(i, i ^ 1) for i in range(rows)]
    f32, bf16 = jnp.float32, jnp.bfloat16
    shape = jax.ShapeDtypeStruct

    def exchange(tensor, pieces):
        return lax.all_to_all(
            tensor.reshape(pairs, pieces, 2, LANES), both_axes, 0, 0,
            tiled=True, axis_index_groups=same_core,
        )

    with jax.named_scope("pack"):
        outgoing = call(
            pack_kernel, shape((10 * channels, LANES), bf16),
            [pltpu.VMEM((channels, length), bf16)] * 2
            + [pltpu.VMEM((4, 2 * channels + SPARE, LANES), f32),
               pltpu.VMEM((10 * channels + SPARE, LANES), f32),
               pltpu.VMEM((10 * channels, LANES), bf16), pltpu.SemaphoreType.DMA((2 + 2 * CHUNKS,))],
            58, 3, True,
        )(k_proj, v_proj, filter_spectrum.reshape(4, 2 * channels, LANES))
    constants, backward = tables(groups, rows, length)
    constants = [jnp.asarray(table) for table in constants]
    outgoing, constants = lax.optimization_barrier((outgoing, constants))
    with jax.named_scope("to_channels"):
        incoming = exchange(outgoing, 5)
    with jax.named_scope("tables"):
        local = [shape(t.shape[1:], t.dtype) for t in constants[:-1]]
        local.append(shape(constants[-1].shape, constants[-1].dtype))
        parts = call(
            tables_kernel, local, [pltpu.SemaphoreType.DMA((len(local),))], 12, len(local)
        )(*constants)
    incoming, parts = lax.optimization_barrier((incoming, parts))
    forward, fine, coarse, mixed = parts
    with jax.named_scope("signal_swap"):
        other = lax.ppermute(incoming[:, 4].reshape(2 * pairs, LANES), "row", swap)
    with jax.named_scope("own_positions"):
        field, response, twist = call(
            own_kernel,
            [shape((4 * pairs, length), f32), shape((2, 2 * pairs, length), f32),
             shape((2, 2 * pairs, length + LANES), f32)],
            [pltpu.VMEM((10 * pairs + SPARE, LANES), f32)], 8,
        )(incoming.reshape(10 * pairs, LANES), forward, fine, coarse)
    with jax.named_scope("spectrum"):
        sent, kept = call(
            spectrum_kernel, [shape((pairs, length), f32)] * 2,
            [pltpu.VMEM((2 * pairs + SPARE, LANES), f32), pltpu.VMEM(backward.shape[1:], bf16),
             pltpu.SemaphoreType.DMA], 20, 1, operands=7,
        )(jnp.asarray(backward), other, forward, field, response, twist, mixed)
    with jax.named_scope("result_swap"):
        came = lax.ppermute(sent, "row", swap)
    with jax.named_scope("add_cores"):
        result = call(
            add_kernel, shape((2 * pairs, LANES), bf16),
            [pltpu.VMEM((2 * pairs + SPARE, LANES), f32)], 4
        )(kept, came)
    with jax.named_scope("to_positions"):
        returned = exchange(result, 1)
    with jax.named_scope("gate"):
        return call(
            gate_kernel, shape((channels, length), f32),
            [pltpu.VMEM((2 * channels + SPARE, LANES), f32), pltpu.VMEM((channels, length), f32),
             pltpu.SemaphoreType.DMA((CHUNKS,))], 4, out_anywhere=True,
        )(returned.reshape(2 * channels, LANES), q_proj, k_proj, v_proj, skip_gain[:, None])


def solution(mesh):
    placed = (
        P(None, ("grp", "row")),
        P(None, ("grp", "row")),
        P(None, ("grp", "row")),
        P(None, "grp", None, "row", None),
        P(),
    )
    return jax.shard_map(
        body, mesh=mesh, in_specs=placed, out_specs=P(None, ("grp", "row")), check_vma=False
    )
```
